32 devices in a mesh: gx: 4 (over z), gy: 8 (over y, x, core).
Axes of the slice: x: 2, y: 2, z: 4, core: 2. Of those that a mesh axis runs over, the one named last changes fastest.
Arguments:
- control: float32 [16, 1024, 512], P(None, 'gy', 'gx'), may hold values from -6 to 6
- scale_x: float32 [16, 512], replicated, may hold values from 2 to 384
- scale_y: float32 [16, 1024], P(None, 'gy'), may hold values from 2 to 384
- vertical_taps: float32 [5, 16], replicated, may hold values from 0.1 to 0.5
Outputs:
- increment: float32 [16, 1024, 512], P(None, 'gy', 'gx')
The draws below stay inside these ranges and needn't reach their ends.
All inputs are finite; a program needn't handle non-finite values.
Results may differ from the reference program's by a relative error of at most 0.00016.
Values sent between devices are 32-bit elements; how exact they have to be, the bound alone decides.
A program may use at most 64 MiB of HBM per device.

```python
import math
import jax
import jax.numpy as jnp
from jax import lax

L = 16
CX = 128
CY = 128
NX = 512
NY = 1024


def level_base(key, count, upper):
    order = jax.random.permutation(jax.random.fold_in(key, 11), count)
    rank = order.astype(jnp.float32) / float(max(count - 1, 1))
    return 3.5 * jnp.power(jnp.float32(upper / 3.5), rank)


def spread_factor(key, count, length):
    return jnp.exp(jax.random.uniform(jax.random.fold_in(key, 23), (count, length), jnp.float32, math.log(0.7), math.log(1.4)))


def draw_scale_x(key, part):
    own_key = jax.random.fold_in(key, 101)
    base = level_base(own_key, L, 2.0 * CX)
    factor = spread_factor(own_key, L, NX)
    return (base[:, None] * factor).astype(jnp.float32)


def draw_scale_y(key, part):
    own_key = jax.random.fold_in(key, 202)
    base = level_base(own_key, L, 2.0 * CY)
    factor = spread_factor(own_key, L, NY)
    return (base[:, None] * factor).astype(jnp.float32)


def level_of(key, dims, shards, low, high):
    level, own = 1.0, jax.random.fold_in(key, 6)
    for dim, parts in shards:
        heights = jnp.exp(jax.random.uniform(jax.random.fold_in(own, dim), (parts,), jnp.float32, low / len(shards), high / len(shards)))
        level = level * jnp.repeat(heights, dims[dim] // parts).reshape([-1 if axis == dim else 1 for axis in range(len(dims))])
    return level


def noise(stream_key, dims, scale, most, split=(), held_as=jnp.bfloat16):
    values = scale * jax.random.normal(stream_key, dims, jnp.float32)
    if split:
        values = values * level_of(stream_key, dims, split, -0.22, 0.18)
    return jnp.clip(values, -most, most).astype(held_as)


def setup_inputs(seed: int = 0) -> dict:
    splits = jax.random.split(jax.random.key(seed), 5)
    control = noise(splits[0], (L, NY, NX), 1.0, 6.0, ((1, 8), (2, 4)), jnp.float32)
    scale_x = draw_scale_x(jax.random.fold_in(splits[4], 71), 0)
    scale_y = draw_scale_y(jax.random.fold_in(splits[4], 71), 0)
    vertical_taps = jnp.clip(jax.random.uniform(splits[3], (5, L), jnp.float32, 0.1, 0.5), 0.1, 0.5)
    return {"control": control, "scale_x": scale_x, "scale_y": scale_y, "vertical_taps": vertical_taps}


def sweep_last(values, damping):
    moved = jnp.moveaxis(values, 2, 0)
    poles_first = jnp.moveaxis(damping, 1, 0)

    def advance(states, item):
        inflow, factor = item
        factor = factor[:, None]
        first = factor * states[0] + (1.0 - factor) * inflow
        second = factor * states[1] + (1.0 - factor) * first
        third = factor * states[2] + (1.0 - factor) * second
        fourth = factor * states[3] + (1.0 - factor) * third
        return ((first, second, third, fourth), fourth)
    blanks = jnp.zeros(moved.shape[1:], jnp.float32)
    _, result = lax.scan(advance, (blanks, blanks, blanks, blanks), (moved, poles_first))
    return jnp.moveaxis(result, 0, 2)

def both_ways(values, damping):
    forward = sweep_last(values, damping)
    return jnp.flip(sweep_last(jnp.flip(forward, 2), jnp.flip(damping, 1)), 2)

def reference(control, scale_x, scale_y, vertical_taps):
    pole_x = jnp.exp(-1.0 / scale_x)
    pole_y = jnp.exp(-1.0 / scale_y)
    values = control * jnp.sqrt(8.0 * scale_x)[:, None, :]
    values = both_ways(values, pole_x)
    values = values * jnp.sqrt(8.0 * scale_y)[:, :, None]
    turned = jnp.swapaxes(values, 1, 2)
    turned = both_ways(turned, pole_y)
    values = jnp.swapaxes(turned, 1, 2)
    levels = values.shape[0]
    padded = jnp.pad(values, ((2, 2), (0, 0), (0, 0)))
    increment = jnp.zeros_like(values)
    for offset in range(5):
        increment = increment + vertical_taps[offset][:, None, None] * padded[offset:offset + levels]
    return increment
```

```python
import functools

import jax
import jax.numpy as jnp
from jax import lax
from jax.experimental import pallas as pl
from jax.experimental.pallas import tpu as pltpu
from jax.sharding import PartitionSpec as P

MESH = pl.DeviceIdType.MESH
UNROLL = 8


def solvers(peers, levels):
    count = min(peers, levels)
    return count, levels // count


def sweep(streams, count, reverse):
    def body(t, carry):
        i = count - 1 - t if reverse else t
        new = []
        for (load, store, _), states in zip(streams, carry):
            pole, entry = load(i)
            keep = 1.0 - pole
            first = pole * states[0]
            if entry is not None:
                value, gain = entry
                first = first + (keep if gain is None else gain) * value
            second = pole * states[1] + keep * first
            third = pole * states[2] + keep * second
            fourth = pole * states[3] + keep * third
            store(i, fourth)
            new.append((first, second, third, fourth))
        return tuple(new)

    start = tuple(tuple(init) for _, _, init in streams)
    return lax.fori_loop(0, count, body, start, unroll=UNROLL)


def send(axis, peers, reach, src, dst, ssem, rsem):
    me = lax.axis_index(axis)
    for offset in range(1, peers):
        peer = lax.rem(me + offset, peers)

        def go(peer=peer):
            pltpu.make_async_remote_copy(
                src_ref=src(peer),
                dst_ref=dst(me),
                send_sem=ssem.at[peer],
                recv_sem=rsem.at[me],
                device_id={axis: peer},
                device_id_type=MESH,
            ).start()

        if reach == peers:
            go()
        else:
            pl.when(reach_of(reach, peer, me))(go)


def reach_of(reach, peer, me):
    count, who = reach if isinstance(reach, tuple) else (reach, "peer")
    return (peer if who == "peer" else me) < count


def settle(axis, peers, reach, src, dst, ssem, rsem, received):
    me = lax.axis_index(axis)
    for offset in range(1, peers):
        peer = lax.rem(me + offset, peers)

        def go(peer=peer):
            copy = pltpu.make_async_remote_copy(
                src_ref=src(peer),
                dst_ref=dst(peer),
                send_sem=ssem.at[peer],
                recv_sem=rsem.at[peer],
                device_id={axis: peer},
                device_id_type=MESH,
            )
            if received:
                copy.wait_recv()
            else:
                copy.wait_send()

        if reach == peers:
            go()
        else:
            pl.when(reach_of(reach, peer, me))(go)


def solve(links, closing, entering, peers, share):
    row = lax.broadcasted_iota(jnp.int32, (8, 128), 0)
    for s in range(share):
        rows = slice(8 * s, 8 * s + 8)
        low = jnp.zeros((8, 128), jnp.float32)
        lows, outs = [], []
        for k in range(peers):
            link = links[k, rows, :]
            out = closing[k, rows, :]
            if k > 0:
                for j in range(4):
                    out = out + link[:, j : j + 1] * low[j : j + 1, :]
            lows.append(low)
            outs.append(out)
            low = out
        high = jnp.zeros((8, 128), jnp.float32)
        for k in reversed(range(peers)):
            entering[k, rows, :] = jnp.where(row < 4, lows[k], high)
            out = outs[k]
            if k < peers - 1:
                link = links[k, rows, :]
                for j in range(4, 8):
                    out = out + link[:, j : j + 1] * high[j : j + 1, :]
            high = out


def correction(basis, entering, level, levels, length):
    wide = basis[pl.ds(level, length, stride=levels), :]
    lane = lax.broadcasted_iota(jnp.int32, wide.shape, 1)
    head = wide.astype(jnp.bfloat16).astype(jnp.float32)
    left = jnp.where(lane < 16, head, wide - head).astype(jnp.bfloat16)[:, :32]
    state = entering[8 * level : 8 * level + 8, :]
    state_head = state.astype(jnp.bfloat16).astype(jnp.float32)
    right = jnp.concatenate(
        [state_head, state - state_head, state_head, jnp.zeros_like(state)], axis=0
    ).astype(jnp.bfloat16)
    return jnp.dot(left, right, preferred_element_type=jnp.float32)


def kernel(
    nx, ny, control, scale_x, scale_y, out,
    vin, px, py, gy, xt, ubx, uby, z, yt,
    lx, ly, sx, sy, ex, ey, glx, gly, gsx, gsy, rx, ry,
    in_sem, xs, xr, ys, yr,
):
    levels, rows, cols = out.shape
    mx, my = lax.axis_index("gx"), lax.axis_index("gy")
    solve_x, share_x = solvers(nx, levels)
    solve_y, share_y = solvers(ny, levels)

    fetch = pltpu.make_async_copy(control, vin, in_sem)
    fetch.start()
    barrier = pltpu.get_barrier_semaphore()
    for axis, mine, peers in (("gx", mx, nx), ("gy", my, ny)):
        for offset in range(1, peers):
            pl.semaphore_signal(
                barrier, inc=1, device_id={axis: lax.rem(mine + offset, peers)}, device_id_type=MESH
            )

    own_x = scale_x[:, pl.ds(pl.multiple_of(mx * cols, cols), cols)]
    own_y = scale_y[...]
    pole_x = jnp.exp(-1.0 / own_x)
    pole_y = jnp.exp(-1.0 / own_y)
    gain_x = jnp.sqrt(8.0 * own_x)
    gain_y = (1.0 - pole_y) * jnp.sqrt(8.0 * own_y)
    for i in range(cols):
        px[i * levels : (i + 1) * levels, :] = jnp.broadcast_to(pole_x[:, i : i + 1], (levels, 128))
    for i in range(rows):
        py[i * levels : (i + 1) * levels, :] = jnp.broadcast_to(pole_y[:, i : i + 1], (levels, 128))
        gy[i * levels : (i + 1) * levels, :] = jnp.broadcast_to(gain_y[:, i : i + 1], (levels, 128))

    def at(i):
        return pl.ds(pl.multiple_of(i * levels, levels), levels)

    def put(ref):
        def store(i, value):
            ref[at(i), :] = value
        return store

    lane = lax.broadcasted_iota(jnp.int32, (levels, 128), 1) % 8
    fore = [(lane == k).astype(jnp.float32) for k in range(4)]
    back = [(lane == k + 4).astype(jnp.float32) for k in range(4)]
    blank = [jnp.zeros((levels, 128), jnp.float32)] * 4

    def keep_states(ref, first, states):
        for k in range(4):
            ref[pl.ds(first + k, levels, stride=8), :] = states[k]

    end_x, end_y = sweep(
        [
            (lambda i: (px[at(i), :], None), put(ubx), fore),
            (lambda i: (py[at(i), :], None), put(uby), fore),
        ],
        cols, False,
    )
    keep_states(lx, 0, end_x)
    keep_states(ly, 0, end_y)
    end_x, end_y = sweep(
        [
            (lambda i: (px[at(i), :], (ubx[at(i), :], None)), put(ubx), back),
            (lambda i: (py[at(i), :], (uby[at(i), :], None)), put(uby), back),
        ],
        cols, True,
    )
    keep_states(lx, 4, end_x)
    keep_states(ly, 4, end_y)

    pl.semaphore_wait(barrier, nx + ny - 2)

    def part(ref, share):
        return lambda peer: ref.at[pl.ds(pl.multiple_of(peer * share * 8, 8), share * 8), :]

    def slot(ref):
        return lambda peer: ref.at[peer]

    to_x = nx if solve_x == nx else (solve_x, "peer")
    at_x = nx if solve_x == nx else (solve_x, "me")
    to_y = ny if solve_y == ny else (solve_y, "peer")
    at_y = ny if solve_y == ny else (solve_y, "me")

    def plan(axis, peers, share, to, own, ssem, rsem, links, glinks, states, gstates, solved, entering):
        return [
            (axis, peers, to, own, part(links, share), slot(glinks), ssem.at[0], rsem.at[0]),
            (axis, peers, to, own, part(states, share), slot(gstates), ssem.at[1], rsem.at[1]),
            (axis, peers, own, to, slot(solved), part(entering, share), ssem.at[2], rsem.at[2]),
        ]

    plan_x = plan("gx", nx, share_x, to_x, at_x, xs, xr, lx, glx, sx, gsx, rx, ex)
    plan_y = plan("gy", ny, share_y, to_y, at_y, ys, yr, ly, gly, sy, gsy, ry, ey)

    def begin(p):
        axis, peers, sending, _, src, dst, ssem, rsem = p
        send(axis, peers, sending, src, dst, ssem, rsem)

    def landed(p):
        axis, peers, _, receiving, src, dst, ssem, rsem = p
        settle(axis, peers, receiving, src, dst, ssem, rsem, True)

    def left(p):
        axis, peers, sending, _, src, dst, ssem, rsem = p
        settle(axis, peers, sending, src, dst, ssem, rsem, False)

    begin(plan_x[0])
    begin(plan_y[0])

    fetch.wait()
    for l in range(levels):
        xt[pl.ds(l, cols, stride=levels), :] = (vin[l] * gain_x[l : l + 1, :]).T
    (end,) = sweep([(lambda i: (px[at(i), :], (xt[at(i), :], None)), put(xt), blank)], cols, False)
    keep_states(sx, 0, end)
    (end,) = sweep([(lambda i: (px[at(i), :], (xt[at(i), :], None)), put(xt), blank)], cols, True)
    keep_states(sx, 4, end)

    def entering_of(plan_, mine, peers, count, share, links, glinks, states, gstates, solved, entering):
        begin(plan_[1])

        def work():
            own = pl.ds(pl.multiple_of(mine * share * 8, 8), share * 8)
            glinks[mine] = links[own, :]
            gstates[mine] = states[own, :]

        def resolve():
            own = pl.ds(pl.multiple_of(mine * share * 8, 8), share * 8)
            solve(glinks, gstates, solved, peers, share)
            entering[own, :] = solved[mine]

        def run(f):
            if count == peers:
                f()
            else:
                pl.when(mine < count)(f)

        run(work)
        landed(plan_[0])
        landed(plan_[1])
        run(resolve)
        begin(plan_[2])
        landed(plan_[2])

    entering_of(plan_x, mx, nx, solve_x, share_x, lx, glx, sx, gsx, rx, ex)
    for l in range(levels):
        full = xt[pl.ds(l, cols, stride=levels), :] + correction(ubx, ex, l, levels, cols)
        z[l * rows : (l + 1) * rows, :] = full.T

    (end,) = sweep(
        [(lambda i: (py[at(i), :], (z[pl.ds(i, levels, stride=rows), :], gy[at(i), :])), put(yt), blank)],
        rows, False,
    )
    keep_states(sy, 0, end)
    (end,) = sweep([(lambda i: (py[at(i), :], (yt[at(i), :], None)), put(yt), blank)], rows, True)
    keep_states(sy, 4, end)

    entering_of(plan_y, my, ny, solve_y, share_y, ly, gly, sy, gsy, ry, ey)
    for l in range(levels):
        out[l] = yt[pl.ds(l, rows, stride=levels), :] + correction(uby, ey, l, levels, rows)

    for p in plan_x + plan_y:
        left(p)


def shards(control, scale_x, scale_y, vertical_taps):
    levels, rows, cols = control.shape
    nx, ny = lax.axis_size("gx"), lax.axis_size("gy")
    _, share_x = solvers(nx, levels)
    _, share_y = solvers(ny, levels)
    f32 = jnp.float32

    def flat(n):
        return pltpu.VMEM((n, 128), f32)

    values = pl.pallas_call(
        functools.partial(kernel, nx, ny),
        out_shape=jax.ShapeDtypeStruct((levels, rows, cols), f32),
        in_specs=[
            pl.BlockSpec(memory_space=pl.ANY),
            pl.BlockSpec(memory_space=pltpu.VMEM),
            pl.BlockSpec(memory_space=pltpu.VMEM),
        ],
        out_specs=pl.BlockSpec(memory_space=pltpu.VMEM),
        scratch_shapes=[
            pltpu.VMEM((levels, rows, cols), f32),
            flat(cols * levels), flat(rows * levels), flat(rows * levels),
            flat(cols * levels), flat(cols * levels), flat(rows * levels),
            flat(levels * rows), flat(rows * levels),
            flat(levels * 8), flat(levels * 8), flat(levels * 8), flat(levels * 8),
            flat(levels * 8), flat(levels * 8),
            pltpu.VMEM((nx, share_x * 8, 128), f32), pltpu.VMEM((ny, share_y * 8, 128), f32),
            pltpu.VMEM((nx, share_x * 8, 128), f32), pltpu.VMEM((ny, share_y * 8, 128), f32),
            pltpu.VMEM((nx, share_x * 8, 128), f32), pltpu.VMEM((ny, share_y * 8, 128), f32),
            pltpu.SemaphoreType.DMA,
            pltpu.SemaphoreType.DMA((3, nx)), pltpu.SemaphoreType.DMA((3, nx)),
            pltpu.SemaphoreType.DMA((3, ny)), pltpu.SemaphoreType.DMA((3, ny)),
        ],
        compiler_params=pltpu.CompilerParams(
            collective_id=0, has_side_effects=True, vmem_limit_bytes=32 * 1024 * 1024
        ),
    )(control, scale_x, scale_y)
    padded = jnp.pad(values, ((2, 2), (0, 0), (0, 0)))
    increment = jnp.zeros_like(values)
    for offset in range(5):
        increment = (
            increment + vertical_taps[offset][:, None, None] * padded[offset : offset + levels]
        )
    return increment


def solution(mesh):
    return jax.shard_map(
        shards,
        mesh=mesh,
        in_specs=(P(None, "gy", "gx"), P(), P(None, "gy"), P()),
        out_specs=P(None, "gy", "gx"),
        check_vma=False,
    )
```

```python
import functools

import jax
import jax.numpy as jnp
from jax import lax
from jax.experimental import pallas as pl
from jax.experimental.pallas import tpu as pltpu
from jax.sharding import PartitionSpec as P

MESH = pl.DeviceIdType.MESH
UNROLL = 8


def sweep(streams, count, reverse):
    def body(t, carry):
        i = count - 1 - t if reverse else t
        new = []
        for (load, store, _), states in zip(streams, carry):
            pole, entry = load(i)
            keep = 1.0 - pole
            first = pole * states[0]
            if entry is not None:
                value, gain = entry
                first = first + (keep if gain is None else gain) * value
            second = pole * states[1] + keep * first
            third = pole * states[2] + keep * second
            fourth = pole * states[3] + keep * third
            store(i, fourth)
            new.append((first, second, third, fourth))
        return tuple(new)

    start = tuple(tuple(init) for _, _, init in streams)
    return lax.fori_loop(0, count, body, start, unroll=UNROLL)


def each_peer(axis, peers, only, act):
    me = lax.axis_index(axis)
    for offset in range(1, peers):
        peer = lax.rem(me + offset, peers)
        if only is None:
            act(me, peer)
        else:
            pl.when(only(me, peer))(functools.partial(act, me, peer))


class Gather:
    def __init__(self, axis, peers, src, dst, ssem, rsem, downward=False):
        self.axis, self.peers, self.src, self.dst = axis, peers, src, dst
        self.ssem, self.rsem, self.downward = ssem, rsem, downward

    def copy(self, slot, peer):
        return pltpu.make_async_remote_copy(
            src_ref=self.src,
            dst_ref=self.dst.at[slot],
            send_sem=self.ssem.at[peer],
            recv_sem=self.rsem.at[slot],
            device_id={self.axis: peer},
            device_id_type=MESH,
        )

    def below(self):
        return (lambda me, peer: peer < me) if self.downward else None

    def above(self):
        return (lambda me, peer: peer > me) if self.downward else None

    def begin(self):
        each_peer(self.axis, self.peers, self.below(), lambda me, peer: self.copy(me, peer).start())

    def landed(self):
        each_peer(self.axis, self.peers, self.above(), lambda me, peer: self.copy(peer, peer).wait_recv())

    def left(self):
        each_peer(self.axis, self.peers, self.below(), lambda me, peer: self.copy(me, peer).wait_send())


def pack(links, lane):
    packed = links[0]
    for k in range(1, 8):
        packed = jnp.where(lane // 8 == k, links[k], packed)
    return packed


def solve(me, peers, links, fore, back, entering, levels):
    shape = (levels, 128)
    low = [jnp.zeros(shape, jnp.float32)] * 4
    mine = low
    outs = []

    def state(ref, k, n):
        return ref[k, n * levels : (n + 1) * levels, :]

    for k in range(peers):
        link = links[k]

        def weight(n, j):
            return jnp.broadcast_to(link[:, 8 * n + j : 8 * n + j + 1], shape)

        mine = [jnp.where(k == me, a, b) for a, b in zip(low, mine)]
        out = [state(back, k, n) for n in range(4)]
        nxt = [state(fore, k, n) for n in range(4)]
        if k > 0:
            for n in range(4):
                for j in range(4):
                    out[n] = out[n] + weight(4 + n, j) * low[j]
            run = [weight(n, 0) for n in range(4)]
            for n in range(4):
                for j in range(n + 1):
                    nxt[n] = nxt[n] + run[n - j] * low[j]
        outs.append(out)
        low = nxt
    high = [jnp.zeros(shape, jnp.float32)] * 4
    for k in range(peers - 1, 0, -1):
        link = links[k]
        run = [jnp.broadcast_to(link[:, 8 * (4 + n) + 4 : 8 * (4 + n) + 5], shape) for n in range(4)]
        new = list(outs[k])
        for n in range(4):
            for j in range(n + 1):
                new[n] = new[n] + run[n - j] * high[j]
        high = [jnp.where(k > me, a, b) for a, b in zip(new, high)]
    for n in range(4):
        entering[n * levels : (n + 1) * levels, :] = mine[n]
        entering[(4 + n) * levels : (5 + n) * levels, :] = high[n]


def right_side(entering, level, levels):
    state = entering[pl.ds(level, 8, stride=levels), :]
    first = state.astype(jnp.bfloat16).astype(jnp.float32)
    return jnp.concatenate(
        [first, state - first, first, jnp.zeros_like(state)], axis=0
    ).astype(jnp.bfloat16)


def split_parts(wide, group):
    first = wide.astype(jnp.bfloat16).astype(jnp.float32)
    return jnp.where(group < 16, first, wide - first).astype(jnp.bfloat16)


def kernel(
    nx, ny, control, scale_x, scale_y, out,
    vin, px, py, gy, xt, ubx, uby, z, yt, vx, vy,
    lx, ly, fx, bx, fy, by, ex, ey, glx, gly, gfx, gbx, gfy, gby,
    in_sem, xs, xr, ys, yr,
):
    levels, rows, cols = out.shape
    mx, my = lax.axis_index("gx"), lax.axis_index("gy")

    fetch = pltpu.make_async_copy(control, vin, in_sem)
    fetch.start()
    gbx[...] = jnp.zeros(gbx.shape, jnp.float32)
    gby[...] = jnp.zeros(gby.shape, jnp.float32)
    barrier = pltpu.get_barrier_semaphore()
    for axis, mine, peers in (("gx", mx, nx), ("gy", my, ny)):
        for offset in range(1, peers):
            pl.semaphore_signal(
                barrier, inc=1, device_id={axis: lax.rem(mine + offset, peers)}, device_id_type=MESH
            )

    own_x = scale_x[:, pl.ds(pl.multiple_of(mx * cols, cols), cols)]
    own_y = scale_y[...]
    pole_x = jnp.exp(-1.0 / own_x)
    pole_y = jnp.exp(-1.0 / own_y)
    gain_x = jnp.sqrt(8.0 * own_x)
    gain_y = (1.0 - pole_y) * jnp.sqrt(8.0 * own_y)
    for i in range(cols):
        px[i * levels : (i + 1) * levels, :] = jnp.broadcast_to(pole_x[:, i : i + 1], (levels, 128))
    for i in range(rows):
        py[i * levels : (i + 1) * levels, :] = jnp.broadcast_to(pole_y[:, i : i + 1], (levels, 128))
        gy[i * levels : (i + 1) * levels, :] = jnp.broadcast_to(gain_y[:, i : i + 1], (levels, 128))

    def at(i):
        return pl.ds(pl.multiple_of(i * levels, levels), levels)

    def put(ref):
        def store(i, value):
            ref[at(i), :] = value
        return store

    lane = lax.broadcasted_iota(jnp.int32, (levels, 128), 1)
    fore = [(lane % 8 == k).astype(jnp.float32) for k in range(4)]
    back = [(lane % 8 == k + 4).astype(jnp.float32) for k in range(4)]
    blank = [jnp.zeros((levels, 128), jnp.float32)] * 4

    def keep_states(ref, states):
        for k in range(4):
            ref[k * levels : (k + 1) * levels, :] = states[k]

    fore_x, fore_y = sweep(
        [
            (lambda i: (px[at(i), :], None), put(ubx), fore),
            (lambda i: (py[at(i), :], None), put(uby), fore),
        ],
        cols, False,
    )
    back_x, back_y = sweep(
        [
            (lambda i: (px[at(i), :], (ubx[at(i), :], None)), put(ubx), back),
            (lambda i: (py[at(i), :], (uby[at(i), :], None)), put(uby), back),
        ],
        cols, True,
    )
    lx[...] = pack(list(fore_x) + list(back_x), lane)
    ly[...] = pack(list(fore_y) + list(back_y), lane)

    pl.semaphore_wait(barrier, nx + ny - 2)

    links_x = Gather("gx", nx, lx, glx, xs.at[0], xr.at[0])
    fores_x = Gather("gx", nx, fx, gfx, xs.at[1], xr.at[1])
    backs_x = Gather("gx", nx, bx, gbx, xs.at[2], xr.at[2], True)
    links_y = Gather("gy", ny, ly, gly, ys.at[0], yr.at[0])
    fores_y = Gather("gy", ny, fy, gfy, ys.at[1], yr.at[1])
    backs_y = Gather("gy", ny, by, gby, ys.at[2], yr.at[2], True)
    links_x.begin()
    links_y.begin()

    fetch.wait()
    for l in range(levels):
        xt[pl.ds(l, cols, stride=levels), :] = (vin[l] * gain_x[l : l + 1, :]).T
    (end,) = sweep([(lambda i: (px[at(i), :], (xt[at(i), :], None)), put(xt), blank)], cols, False)
    keep_states(fx, end)
    fores_x.begin()
    (end,) = sweep([(lambda i: (px[at(i), :], (xt[at(i), :], None)), put(xt), blank)], cols, True)
    keep_states(bx, end)
    backs_x.begin()

    group = lax.broadcasted_iota(jnp.int32, (32, 128), 0)
    for l in range(levels):
        z[l * rows : (l + 1) * rows, :] = xt[pl.ds(l, cols, stride=levels), :].T
        wide = ubx[pl.ds(l, cols, stride=levels), :]
        vx[l * 32 : (l + 1) * 32, :] = split_parts(wide.T[:32, :], group)
    glx[mx] = lx[...]
    gfx[mx] = fx[...]
    gbx[mx] = bx[...]
    links_x.landed()
    fores_x.landed()
    backs_x.landed()
    solve(mx, nx, glx, gfx, gbx, ex, levels)
    for l in range(levels):
        z[l * rows : (l + 1) * rows, :] = z[l * rows : (l + 1) * rows, :] + lax.dot_general(
            right_side(ex, l, levels),
            vx[l * 32 : (l + 1) * 32, :],
            (((0,), (0,)), ((), ())),
            preferred_element_type=jnp.float32,
        )

    (end,) = sweep(
        [(lambda i: (py[at(i), :], (z[pl.ds(i, levels, stride=rows), :], gy[at(i), :])), put(yt), blank)],
        rows, False,
    )
    keep_states(fy, end)
    fores_y.begin()
    (end,) = sweep([(lambda i: (py[at(i), :], (yt[at(i), :], None)), put(yt), blank)], rows, True)
    keep_states(by, end)
    backs_y.begin()

    group = lax.broadcasted_iota(jnp.int32, (rows, 128), 1)
    for l in range(levels):
        vy[l * rows : (l + 1) * rows, :] = split_parts(uby[pl.ds(l, rows, stride=levels), :], group)
    gly[my] = ly[...]
    gfy[my] = fy[...]
    gby[my] = by[...]
    links_y.landed()
    fores_y.landed()
    backs_y.landed()
    solve(my, ny, gly, gfy, gby, ey, levels)
    for l in range(levels):
        out[l] = yt[pl.ds(l, rows, stride=levels), :] + jnp.dot(
            vy[l * rows : (l + 1) * rows, :][:, :32],
            right_side(ey, l, levels),
            preferred_element_type=jnp.float32,
        )

    for gather in (links_x, fores_x, backs_x, links_y, fores_y, backs_y):
        gather.left()


def band(taps, values, out, buffer, sems):
    levels = values.shape[0]
    copies = []
    for l in range(levels):
        total = None
        for d in range(5):
            if 0 <= l + d - 2 < levels:
                term = taps[d, l] * values[l + d - 2]
                total = term if total is None else total + term
        buffer[l] = total
        copies.append(pltpu.make_async_copy(buffer.at[l], out.at[l], sems.at[l]))
        copies[-1].start()
    for copy in copies:
        copy.wait()


def shards(control, scale_x, scale_y, vertical_taps):
    levels, rows, cols = control.shape
    nx, ny = lax.axis_size("gx"), lax.axis_size("gy")
    f32 = jnp.float32

    def flat(n, dtype=f32):
        return pltpu.VMEM((n, 128), dtype)

    def slots(n, height):
        return pltpu.VMEM((n, height, 128), f32)

    values = pl.pallas_call(
        functools.partial(kernel, nx, ny),
        out_shape=jax.ShapeDtypeStruct((levels, rows, cols), f32),
        in_specs=[
            pl.BlockSpec(memory_space=pltpu.HBM),
            pl.BlockSpec(memory_space=pltpu.VMEM),
            pl.BlockSpec(memory_space=pltpu.VMEM),
        ],
        out_specs=pl.BlockSpec(memory_space=pltpu.VMEM),
        scratch_shapes=[
            pltpu.VMEM((levels, rows, cols), f32),
            flat(cols * levels), flat(rows * levels), flat(rows * levels),
            flat(cols * levels), flat(cols * levels), flat(rows * levels),
            flat(levels * rows), flat(rows * levels),
            flat(levels * 32, jnp.bfloat16), flat(levels * rows, jnp.bfloat16),
            flat(levels), flat(levels),
            flat(levels * 4), flat(levels * 4), flat(levels * 4), flat(levels * 4),
            flat(levels * 8), flat(levels * 8),
            slots(nx, levels), slots(ny, levels),
            slots(nx, levels * 4), slots(nx, levels * 4),
            slots(ny, levels * 4), slots(ny, levels * 4),
            pltpu.SemaphoreType.DMA,
            pltpu.SemaphoreType.DMA((3, nx)), pltpu.SemaphoreType.DMA((3, nx)),
            pltpu.SemaphoreType.DMA((3, ny)), pltpu.SemaphoreType.DMA((3, ny)),
        ],
        compiler_params=pltpu.CompilerParams(
            collective_id=0, has_side_effects=True, vmem_limit_bytes=32 * 1024 * 1024
        ),
    )(control, scale_x, scale_y)
    return pl.pallas_call(
        band,
        out_shape=jax.ShapeDtypeStruct((levels, rows, cols), f32),
        in_specs=[
            pl.BlockSpec(memory_space=pltpu.SMEM),
            pl.BlockSpec(memory_space=pltpu.VMEM),
        ],
        out_specs=pl.BlockSpec(memory_space=pltpu.HBM),
        scratch_shapes=[
            pltpu.VMEM((levels, rows, cols), f32),
            pltpu.SemaphoreType.DMA((levels,)),
        ],
        compiler_params=pltpu.CompilerParams(vmem_limit_bytes=16 * 1024 * 1024),
    )(vertical_taps, values)


def solution(mesh):
    return jax.shard_map(
        shards,
        mesh=mesh,
        in_specs=(P(None, "gy", "gx"), P(), P(None, "gy"), P()),
        out_specs=P(None, "gy", "gx"),
        check_vma=False,
    )
```

```python
import functools

import jax
import jax.numpy as jnp
from jax import lax
from jax.experimental import pallas as pl
from jax.experimental.pallas import tpu as pltpu
from jax.sharding import PartitionSpec as P

MESH = pl.DeviceIdType.MESH
UNROLL = 128


def sweep(streams, count, reverse):
    def body(t, carry):
        i = count - 1 - t if reverse else t
        new = []
        for (load, store, _), states in zip(streams, carry):
            pole, entry = load(i)
            keep = 1.0 - pole
            first = pole * states[0]
            if entry is not None:
                value, gain = entry
                first = first + (keep if gain is None else gain) * value
            second = pole * states[1] + keep * first
            third = pole * states[2] + keep * second
            fourth = pole * states[3] + keep * third
            store(i, fourth)
            new.append((first, second, third, fourth))
        return tuple(new)

    start = tuple(tuple(init) for _, _, init in streams)
    return lax.fori_loop(0, count, body, start, unroll=UNROLL)


def each_peer(axis, peers, only, act):
    me = lax.axis_index(axis)
    for offset in range(1, peers):
        peer = lax.rem(me + offset, peers)
        if only is None:
            act(me, peer)
        else:
            pl.when(only(me, peer))(functools.partial(act, me, peer))


class Gather:
    def __init__(self, axis, peers, src, dst, ssem, rsem, rule=None):
        self.axis, self.peers, self.src, self.dst = axis, peers, src, dst
        self.ssem, self.rsem, self.rule = ssem, rsem, rule

    def copy(self, slot, peer):
        return pltpu.make_async_remote_copy(
            src_ref=self.src,
            dst_ref=self.dst.at[slot],
            send_sem=self.ssem.at[peer],
            recv_sem=self.rsem.at[slot],
            device_id={self.axis: peer},
            device_id_type=MESH,
        )

    def below(self):
        return self.rule

    def above(self):
        return None if self.rule is None else lambda me, peer: self.rule(peer, me)

    def begin(self):
        each_peer(self.axis, self.peers, self.below(), lambda me, peer: self.copy(me, peer).start())

    def landed(self):
        each_peer(self.axis, self.peers, self.above(), lambda me, peer: self.copy(peer, peer).wait_recv())

    def left(self):
        each_peer(self.axis, self.peers, self.below(), lambda me, peer: self.copy(me, peer).wait_send())


def pack(links, lane):
    packed = links[0]
    for k in range(1, 8):
        packed = jnp.where(lane // 8 == k, links[k], packed)
    return packed


def solve(me, peers, links, fore, back, entering, levels):
    shape = (levels, 128)
    low = [jnp.zeros(shape, jnp.float32)] * 4
    mine = low
    outs = []

    def state(ref, k, n):
        return ref[k, n * levels : (n + 1) * levels, :]

    for k in range(peers):
        link = links[k]

        def weight(n, j):
            return jnp.broadcast_to(link[:, 8 * n + j : 8 * n + j + 1], shape)

        mine = [jnp.where(k == me, a, b) for a, b in zip(low, mine)]
        out = [state(back, k, n) for n in range(4)]
        nxt = [state(fore, k, n) for n in range(4)] if k < peers - 1 else None
        if k > 0:
            for n in range(4):
                for j in range(4):
                    out[n] = out[n] + weight(4 + n, j) * low[j]
        if 0 < k < peers - 1:
            run = [weight(n, 0) for n in range(4)]
            for n in range(4):
                for j in range(n + 1):
                    nxt[n] = nxt[n] + run[n - j] * low[j]
        outs.append(out)
        low = nxt
    high = [jnp.zeros(shape, jnp.float32)] * 4
    for k in range(peers - 1, 0, -1):
        link = links[k]
        run = [jnp.broadcast_to(link[:, 8 * (4 + n) + 4 : 8 * (4 + n) + 5], shape) for n in range(4)]
        new = list(outs[k])
        for n in range(4):
            for j in range(n + 1):
                new[n] = new[n] + run[n - j] * high[j]
        high = [jnp.where(k > me, a, b) for a, b in zip(new, high)]
    for n in range(4):
        entering[n * levels : (n + 1) * levels, :] = mine[n]
        entering[(4 + n) * levels : (5 + n) * levels, :] = high[n]


def right_side(entering, level, levels):
    state = entering[pl.ds(level, 8, stride=levels), :]
    first = state.astype(jnp.bfloat16).astype(jnp.float32)
    return jnp.concatenate(
        [first, state - first, first, jnp.zeros_like(state)], axis=0
    ).astype(jnp.bfloat16)


def split_parts(wide, group):
    first = wide.astype(jnp.bfloat16).astype(jnp.float32)
    return jnp.where(group < 16, first, wide - first).astype(jnp.bfloat16)


def kernel(
    nx, ny, control, scale_x, scale_y, out,
    vin, px, py, gy, xt, ubx, uby, z, yt, vx, vy,
    lx, ly, fx, bx, fy, by, ex, ey, glx, gly, gfx, gbx, gfy, gby,
    in_sem, xs, xr, ys, yr,
):
    levels, rows, cols = out.shape
    mx, my = lax.axis_index("gx"), lax.axis_index("gy")

    fetch = pltpu.make_async_copy(control, vin, in_sem)
    fetch.start()
    gbx[...] = jnp.zeros(gbx.shape, jnp.float32)
    gby[...] = jnp.zeros(gby.shape, jnp.float32)
    barrier = pltpu.get_barrier_semaphore()
    for axis, mine, peers in (("gx", mx, nx), ("gy", my, ny)):
        for offset in range(1, peers):
            pl.semaphore_signal(
                barrier, inc=1, device_id={axis: lax.rem(mine + offset, peers)}, device_id_type=MESH
            )

    own_x = scale_x[:, pl.ds(pl.multiple_of(mx * cols, cols), cols)]
    own_y = scale_y[...]
    pole_x = jnp.exp(-1.0 / own_x)
    pole_y = jnp.exp(-1.0 / own_y)
    gain_x = jnp.sqrt(8.0 * own_x)
    gain_y = (1.0 - pole_y) * jnp.sqrt(8.0 * own_y)
    for i in range(cols):
        px[i * levels : (i + 1) * levels, :] = jnp.broadcast_to(pole_x[:, i : i + 1], (levels, 128))
    for i in range(rows):
        py[i * levels : (i + 1) * levels, :] = jnp.broadcast_to(pole_y[:, i : i + 1], (levels, 128))
        gy[i * levels : (i + 1) * levels, :] = jnp.broadcast_to(gain_y[:, i : i + 1], (levels, 128))

    def at(i):
        return pl.ds(pl.multiple_of(i * levels, levels), levels)

    def put(ref):
        def store(i, value):
            ref[at(i), :] = value
        return store

    lane = lax.broadcasted_iota(jnp.int32, (levels, 128), 1)
    fore = [(lane % 8 == k).astype(jnp.float32) for k in range(4)]
    back = [(lane % 8 == k + 4).astype(jnp.float32) for k in range(4)]
    blank = [jnp.zeros((levels, 128), jnp.float32)] * 4

    def keep_states(ref, states):
        for k in range(4):
            ref[k * levels : (k + 1) * levels, :] = states[k]

    fore_x, fore_y = sweep(
        [
            (lambda i: (px[at(i), :], None), put(ubx), fore),
            (lambda i: (py[at(i), :], None), put(uby), fore),
        ],
        cols, False,
    )
    back_x, back_y = sweep(
        [
            (lambda i: (px[at(i), :], (ubx[at(i), :], None)), put(ubx), back),
            (lambda i: (py[at(i), :], (uby[at(i), :], None)), put(uby), back),
        ],
        cols, True,
    )
    lx[...] = pack(list(fore_x) + list(back_x), lane)
    ly[...] = pack(list(fore_y) + list(back_y), lane)

    pl.semaphore_wait(barrier, nx + ny - 2)

    links_x = Gather("gx", nx, lx, glx, xs.at[0], xr.at[0])
    fores_x = Gather("gx", nx, fx, gfx, xs.at[1], xr.at[1], lambda a, b: a < nx - 1)
    backs_x = Gather("gx", nx, bx, gbx, xs.at[2], xr.at[2], lambda a, b: b < a)
    links_y = Gather("gy", ny, ly, gly, ys.at[0], yr.at[0])
    fores_y = Gather("gy", ny, fy, gfy, ys.at[1], yr.at[1], lambda a, b: a < ny - 1)
    backs_y = Gather("gy", ny, by, gby, ys.at[2], yr.at[2], lambda a, b: b < a)
    links_x.begin()
    links_y.begin()

    fetch.wait()
    for l in range(levels):
        xt[pl.ds(l, cols, stride=levels), :] = (vin[l] * gain_x[l : l + 1, :]).T
    (end,) = sweep([(lambda i: (px[at(i), :], (xt[at(i), :], None)), put(xt), blank)], cols, False)
    keep_states(fx, end)
    fores_x.begin()
    (end,) = sweep([(lambda i: (px[at(i), :], (xt[at(i), :], None)), put(xt), blank)], cols, True)
    keep_states(bx, end)
    backs_x.begin()

    group = lax.broadcasted_iota(jnp.int32, (32, 128), 0)
    for l in range(levels):
        z[l * rows : (l + 1) * rows, :] = xt[pl.ds(l, cols, stride=levels), :].T
        wide = ubx[pl.ds(l, cols, stride=levels), :]
        vx[l * 32 : (l + 1) * 32, :] = split_parts(wide.T[:32, :], group)
    glx[mx] = lx[...]
    gfx[mx] = fx[...]
    gbx[mx] = bx[...]
    links_x.landed()
    fores_x.landed()
    backs_x.landed()
    solve(mx, nx, glx, gfx, gbx, ex, levels)
    for l in range(levels):
        z[l * rows : (l + 1) * rows, :] = z[l * rows : (l + 1) * rows, :] + lax.dot_general(
            right_side(ex, l, levels),
            vx[l * 32 : (l + 1) * 32, :],
            (((0,), (0,)), ((), ())),
            preferred_element_type=jnp.float32,
        )

    (end,) = sweep(
        [(lambda i: (py[at(i), :], (z[pl.ds(i, levels, stride=rows), :], gy[at(i), :])), put(yt), blank)],
        rows, False,
    )
    keep_states(fy, end)
    fores_y.begin()
    (end,) = sweep([(lambda i: (py[at(i), :], (yt[at(i), :], None)), put(yt), blank)], rows, True)
    keep_states(by, end)
    backs_y.begin()

    group = lax.broadcasted_iota(jnp.int32, (rows, 128), 1)
    for l in range(levels):
        vy[l * rows : (l + 1) * rows, :] = split_parts(uby[pl.ds(l, rows, stride=levels), :], group)
    gly[my] = ly[...]
    gfy[my] = fy[...]
    gby[my] = by[...]
    links_y.landed()
    fores_y.landed()
    backs_y.landed()
    solve(my, ny, gly, gfy, gby, ey, levels)
    for l in range(levels):
        out[l] = yt[pl.ds(l, rows, stride=levels), :] + jnp.dot(
            vy[l * rows : (l + 1) * rows, :][:, :32],
            right_side(ey, l, levels),
            preferred_element_type=jnp.float32,
        )

    for gather in (links_x, fores_x, backs_x, links_y, fores_y, backs_y):
        gather.left()


def band(taps, values, out, buffer, sems):
    levels = values.shape[0]
    copies = []
    for l in range(levels):
        total = None
        for d in range(5):
            if 0 <= l + d - 2 < levels:
                term = taps[d, l] * values[l + d - 2]
                total = term if total is None else total + term
        buffer[l] = total
        copies.append(pltpu.make_async_copy(buffer.at[l], out.at[l], sems.at[l]))
        copies[-1].start()
    for copy in copies:
        copy.wait()


def shards(control, scale_x, scale_y, vertical_taps):
    levels, rows, cols = control.shape
    nx, ny = lax.axis_size("gx"), lax.axis_size("gy")
    f32 = jnp.float32

    def flat(n, dtype=f32):
        return pltpu.VMEM((n, 128), dtype)

    def slots(n, height):
        return pltpu.VMEM((n, height, 128), f32)

    values = pl.pallas_call(
        functools.partial(kernel, nx, ny),
        out_shape=jax.ShapeDtypeStruct((levels, rows, cols), f32),
        in_specs=[
            pl.BlockSpec(memory_space=pltpu.HBM),
            pl.BlockSpec(memory_space=pltpu.VMEM),
            pl.BlockSpec(memory_space=pltpu.VMEM),
        ],
        out_specs=pl.BlockSpec(memory_space=pltpu.VMEM),
        scratch_shapes=[
            pltpu.VMEM((levels, rows, cols), f32),
            flat(cols * levels), flat(rows * levels), flat(rows * levels),
            flat(cols * levels), flat(cols * levels), flat(rows * levels),
            flat(levels * rows), flat(rows * levels),
            flat(levels * 32, jnp.bfloat16), flat(levels * rows, jnp.bfloat16),
            flat(levels), flat(levels),
            flat(levels * 4), flat(levels * 4), flat(levels * 4), flat(levels * 4),
            flat(levels * 8), flat(levels * 8),
            slots(nx, levels), slots(ny, levels),
            slots(nx, levels * 4), slots(nx, levels * 4),
            slots(ny, levels * 4), slots(ny, levels * 4),
            pltpu.SemaphoreType.DMA,
            pltpu.SemaphoreType.DMA((3, nx)), pltpu.SemaphoreType.DMA((3, nx)),
            pltpu.SemaphoreType.DMA((3, ny)), pltpu.SemaphoreType.DMA((3, ny)),
        ],
        compiler_params=pltpu.CompilerParams(
            collective_id=0, has_side_effects=True, vmem_limit_bytes=52 * 1024 * 1024
        ),
    )(control, scale_x, scale_y)
    return pl.pallas_call(
        band,
        out_shape=jax.ShapeDtypeStruct((levels, rows, cols), f32),
        in_specs=[
            pl.BlockSpec(memory_space=pltpu.SMEM),
            pl.BlockSpec(memory_space=pltpu.VMEM),
        ],
        out_specs=pl.BlockSpec(memory_space=pltpu.HBM),
        scratch_shapes=[
            pltpu.VMEM((levels, rows, cols), f32),
            pltpu.SemaphoreType.DMA((levels,)),
        ],
        compiler_params=pltpu.CompilerParams(vmem_limit_bytes=16 * 1024 * 1024),
    )(vertical_taps, values)


def solution(mesh):
    return jax.shard_map(
        shards,
        mesh=mesh,
        in_specs=(P(None, "gy", "gx"), P(), P(None, "gy"), P()),
        out_specs=P(None, "gy", "gx"),
        check_vma=False,
    )
```

```python
import functools

import jax
import jax.numpy as jnp
from jax import lax
from jax.experimental import pallas as pl
from jax.experimental.pallas import tpu as pltpu
from jax.sharding import PartitionSpec as P

MESH = pl.DeviceIdType.MESH
UNROLL = 128


def sweep(streams, count, reverse):
    def body(t, carry):
        i = count - 1 - t if reverse else t
        new = []
        for (load, store, _), states in zip(streams, carry):
            pole, entry = load(i)
            keep = 1.0 - pole
            first = pole * states[0]
            if entry is not None:
                value, gain = entry
                first = first + (keep if gain is None else gain) * value
            second = pole * states[1] + keep * first
            third = pole * states[2] + keep * second
            fourth = pole * states[3] + keep * third
            store(i, fourth)
            new.append((first, second, third, fourth))
        return tuple(new)

    start = tuple(tuple(init) for _, _, init in streams)
    return lax.fori_loop(0, count, body, start, unroll=UNROLL)


def each_peer(axis, peers, only, act):
    me = lax.axis_index(axis)
    for offset in range(1, peers):
        peer = lax.rem(me + offset, peers)
        if only is None:
            act(me, peer)
        else:
            pl.when(only(me, peer))(functools.partial(act, me, peer))


class Gather:
    def __init__(self, axis, peers, src, dst, ssem, rsem, rule=None):
        self.axis, self.peers, self.src, self.dst = axis, peers, src, dst
        self.ssem, self.rsem, self.rule = ssem, rsem, rule

    def copy(self, slot, peer):
        return pltpu.make_async_remote_copy(
            src_ref=self.src,
            dst_ref=self.dst.at[slot],
            send_sem=self.ssem.at[peer],
            recv_sem=self.rsem.at[slot],
            device_id={self.axis: peer},
            device_id_type=MESH,
        )

    def below(self):
        return self.rule

    def above(self):
        return None if self.rule is None else lambda me, peer: self.rule(peer, me)

    def begin(self):
        each_peer(self.axis, self.peers, self.below(), lambda me, peer: self.copy(me, peer).start())

    def landed(self):
        each_peer(self.axis, self.peers, self.above(), lambda me, peer: self.copy(peer, peer).wait_recv())

    def left(self):
        each_peer(self.axis, self.peers, self.below(), lambda me, peer: self.copy(me, peer).wait_send())


def pack(links, lane):
    packed = links[0]
    for k in range(1, 8):
        packed = jnp.where(lane // 8 == k, links[k], packed)
    return packed


def solve(me, peers, links, fore, back, entering, levels):
    shape = (levels, 128)
    low = [jnp.zeros(shape, jnp.float32)] * 4
    mine = low
    outs = []

    def state(ref, k, n):
        return ref[k, n * levels : (n + 1) * levels, :]

    for k in range(peers):
        link = links[k]

        def weight(n, j):
            return jnp.broadcast_to(link[:, 8 * n + j : 8 * n + j + 1], shape)

        mine = [jnp.where(k == me, a, b) for a, b in zip(low, mine)]
        out = [state(back, k, n) for n in range(4)]
        nxt = [state(fore, k, n) for n in range(4)] if k < peers - 1 else None
        if k > 0:
            for n in range(4):
                for j in range(4):
                    out[n] = out[n] + weight(4 + n, j) * low[j]
        if 0 < k < peers - 1:
            run = [weight(n, 0) for n in range(4)]
            for n in range(4):
                for j in range(n + 1):
                    nxt[n] = nxt[n] + run[n - j] * low[j]
        outs.append(out)
        low = nxt
    high = [jnp.zeros(shape, jnp.float32)] * 4
    for k in range(peers - 1, 0, -1):
        link = links[k]
        run = [jnp.broadcast_to(link[:, 8 * (4 + n) + 4 : 8 * (4 + n) + 5], shape) for n in range(4)]
        new = list(outs[k])
        for n in range(4):
            for j in range(n + 1):
                new[n] = new[n] + run[n - j] * high[j]
        high = [jnp.where(k > me, a, b) for a, b in zip(new, high)]
    for n in range(4):
        entering[n * levels : (n + 1) * levels, :] = mine[n]
        entering[(4 + n) * levels : (5 + n) * levels, :] = high[n]


def right_side(entering, level, levels):
    state = entering[pl.ds(level, 8, stride=levels), :]
    first = state.astype(jnp.bfloat16).astype(jnp.float32)
    return jnp.concatenate(
        [first, state - first, first, jnp.zeros_like(state)], axis=0
    ).astype(jnp.bfloat16)


def split_parts(wide, group):
    first = wide.astype(jnp.bfloat16).astype(jnp.float32)
    return jnp.where(group < 16, first, wide - first).astype(jnp.bfloat16)


def kernel(
    nx, ny, control, scale_x, scale_y, out,
    vin, px, py, gy, xt, ubx, uby, z, yt, vx, vy,
    lx, ly, fx, bx, fy, by, ex, ey, glx, gly, gfx, gbx, gfy, gby,
    in_sem, xs, xr, ys, yr,
):
    levels, rows, cols = out.shape
    mx, my = lax.axis_index("gx"), lax.axis_index("gy")

    fetch = pltpu.make_async_copy(control, vin, in_sem)
    fetch.start()
    gbx[...] = jnp.zeros(gbx.shape, jnp.float32)
    gby[...] = jnp.zeros(gby.shape, jnp.float32)
    barrier = pltpu.get_barrier_semaphore()
    for axis, mine, peers in (("gx", mx, nx), ("gy", my, ny)):
        for offset in range(1, peers):
            pl.semaphore_signal(
                barrier, inc=1, device_id={axis: lax.rem(mine + offset, peers)}, device_id_type=MESH
            )

    own_x = scale_x[:, pl.ds(pl.multiple_of(mx * cols, cols), cols)]
    own_y = scale_y[...]
    pole_x = jnp.exp(-1.0 / own_x)
    pole_y = jnp.exp(-1.0 / own_y)
    gain_x = jnp.sqrt(8.0 * own_x)
    gain_y = (1.0 - pole_y) * jnp.sqrt(8.0 * own_y)
    for i in range(cols):
        px[i * levels : (i + 1) * levels, :] = jnp.broadcast_to(pole_x[:, i : i + 1], (levels, 128))
    def at(i):
        return pl.ds(pl.multiple_of(i * levels, levels), levels)

    def put(ref):
        def store(i, value):
            ref[at(i), :] = value
        return store

    lane = lax.broadcasted_iota(jnp.int32, (levels, 128), 1)
    fore = [(lane % 8 == k).astype(jnp.float32) for k in range(4)]
    back = [(lane % 8 == k + 4).astype(jnp.float32) for k in range(4)]
    blank = [jnp.zeros((levels, 128), jnp.float32)] * 4

    def keep_states(ref, states):
        for k in range(4):
            ref[k * levels : (k + 1) * levels, :] = states[k]

    links_x = Gather("gx", nx, lx, glx, xs.at[0], xr.at[0])
    fores_x = Gather("gx", nx, fx, gfx, xs.at[1], xr.at[1], lambda a, b: a < nx - 1)
    backs_x = Gather("gx", nx, bx, gbx, xs.at[2], xr.at[2], lambda a, b: b < a)
    links_y = Gather("gy", ny, ly, gly, ys.at[0], yr.at[0])
    fores_y = Gather("gy", ny, fy, gfy, ys.at[1], yr.at[1], lambda a, b: a < ny - 1)
    backs_y = Gather("gy", ny, by, gby, ys.at[2], yr.at[2], lambda a, b: b < a)

    fetch.wait()
    for l in range(levels):
        xt[pl.ds(l, cols, stride=levels), :] = (vin[l] * gain_x[l : l + 1, :]).T
    end, fore_x = sweep(
        [
            (lambda i: (px[at(i), :], (xt[at(i), :], None)), put(xt), blank),
            (lambda i: (px[at(i), :], None), put(ubx), fore),
        ],
        cols, False,
    )
    keep_states(fx, end)
    pl.semaphore_wait(barrier, nx + ny - 2)
    fores_x.begin()
    end, back_x = sweep(
        [
            (lambda i: (px[at(i), :], (xt[at(i), :], None)), put(xt), blank),
            (lambda i: (px[at(i), :], (ubx[at(i), :], None)), put(ubx), back),
        ],
        cols, True,
    )
    keep_states(bx, end)
    lx[...] = pack(list(fore_x) + list(back_x), lane)
    links_x.begin()
    backs_x.begin()

    for i in range(rows):
        py[i * levels : (i + 1) * levels, :] = jnp.broadcast_to(pole_y[:, i : i + 1], (levels, 128))
        gy[i * levels : (i + 1) * levels, :] = jnp.broadcast_to(gain_y[:, i : i + 1], (levels, 128))

    (fore_y,) = sweep([(lambda i: (py[at(i), :], None), put(uby), fore)], rows, False)
    (back_y,) = sweep([(lambda i: (py[at(i), :], (uby[at(i), :], None)), put(uby), back)], rows, True)
    ly[...] = pack(list(fore_y) + list(back_y), lane)
    links_y.begin()

    group = lax.broadcasted_iota(jnp.int32, (32, 128), 0)
    for l in range(levels):
        z[l * rows : (l + 1) * rows, :] = xt[pl.ds(l, cols, stride=levels), :].T
        wide = ubx[pl.ds(l, cols, stride=levels), :]
        vx[l * 32 : (l + 1) * 32, :] = split_parts(wide.T[:32, :], group)
    glx[mx] = lx[...]
    gfx[mx] = fx[...]
    gbx[mx] = bx[...]
    links_x.landed()
    fores_x.landed()
    backs_x.landed()
    solve(mx, nx, glx, gfx, gbx, ex, levels)
    for l in range(levels):
        z[l * rows : (l + 1) * rows, :] = z[l * rows : (l + 1) * rows, :] + lax.dot_general(
            right_side(ex, l, levels),
            vx[l * 32 : (l + 1) * 32, :],
            (((0,), (0,)), ((), ())),
            preferred_element_type=jnp.float32,
        )

    (end,) = sweep(
        [(lambda i: (py[at(i), :], (z[pl.ds(i, levels, stride=rows), :], gy[at(i), :])), put(yt), blank)],
        rows, False,
    )
    keep_states(fy, end)
    fores_y.begin()
    (end,) = sweep([(lambda i: (py[at(i), :], (yt[at(i), :], None)), put(yt), blank)], rows, True)
    keep_states(by, end)
    backs_y.begin()

    group = lax.broadcasted_iota(jnp.int32, (rows, 128), 1)
    for l in range(levels):
        vy[l * rows : (l + 1) * rows, :] = split_parts(uby[pl.ds(l, rows, stride=levels), :], group)
    gly[my] = ly[...]
    gfy[my] = fy[...]
    gby[my] = by[...]
    links_y.landed()
    fores_y.landed()
    backs_y.landed()
    solve(my, ny, gly, gfy, gby, ey, levels)
    for l in range(levels):
        out[l] = yt[pl.ds(l, rows, stride=levels), :] + jnp.dot(
            vy[l * rows : (l + 1) * rows, :][:, :32],
            right_side(ey, l, levels),
            preferred_element_type=jnp.float32,
        )

    for gather in (links_x, fores_x, backs_x, links_y, fores_y, backs_y):
        gather.left()


def band(taps, values, out, buffer, sems):
    levels = values.shape[0]
    copies = []
    for l in range(levels):
        total = None
        for d in range(5):
            if 0 <= l + d - 2 < levels:
                term = taps[d, l] * values[l + d - 2]
                total = term if total is None else total + term
        buffer[l] = total
        copies.append(pltpu.make_async_copy(buffer.at[l], out.at[l], sems.at[l]))
        copies[-1].start()
    for copy in copies:
        copy.wait()


def shards(control, scale_x, scale_y, vertical_taps):
    levels, rows, cols = control.shape
    nx, ny = lax.axis_size("gx"), lax.axis_size("gy")
    f32 = jnp.float32

    def flat(n, dtype=f32):
        return pltpu.VMEM((n, 128), dtype)

    def slots(n, height):
        return pltpu.VMEM((n, height, 128), f32)

    values = pl.pallas_call(
        functools.partial(kernel, nx, ny),
        out_shape=jax.ShapeDtypeStruct((levels, rows, cols), f32),
        in_specs=[
            pl.BlockSpec(memory_space=pltpu.HBM),
            pl.BlockSpec(memory_space=pltpu.VMEM),
            pl.BlockSpec(memory_space=pltpu.VMEM),
        ],
        out_specs=pl.BlockSpec(memory_space=pltpu.VMEM),
        scratch_shapes=[
            pltpu.VMEM((levels, rows, cols), f32),
            flat(cols * levels), flat(rows * levels), flat(rows * levels),
            flat(cols * levels), flat(cols * levels), flat(rows * levels),
            flat(levels * rows), flat(rows * levels),
            flat(levels * 32, jnp.bfloat16), flat(levels * rows, jnp.bfloat16),
            flat(levels), flat(levels),
            flat(levels * 4), flat(levels * 4), flat(levels * 4), flat(levels * 4),
            flat(levels * 8), flat(levels * 8),
            slots(nx, levels), slots(ny, levels),
            slots(nx, levels * 4), slots(nx, levels * 4),
            slots(ny, levels * 4), slots(ny, levels * 4),
            pltpu.SemaphoreType.DMA,
            pltpu.SemaphoreType.DMA((3, nx)), pltpu.SemaphoreType.DMA((3, nx)),
            pltpu.SemaphoreType.DMA((3, ny)), pltpu.SemaphoreType.DMA((3, ny)),
        ],
        compiler_params=pltpu.CompilerParams(
            collective_id=0, has_side_effects=True, vmem_limit_bytes=52 * 1024 * 1024
        ),
    )(control, scale_x, scale_y)
    return pl.pallas_call(
        band,
        out_shape=jax.ShapeDtypeStruct((levels, rows, cols), f32),
        in_specs=[
            pl.BlockSpec(memory_space=pltpu.SMEM),
            pl.BlockSpec(memory_space=pltpu.VMEM),
        ],
        out_specs=pl.BlockSpec(memory_space=pltpu.HBM),
        scratch_shapes=[
            pltpu.VMEM((levels, rows, cols), f32),
            pltpu.SemaphoreType.DMA((levels,)),
        ],
        compiler_params=pltpu.CompilerParams(vmem_limit_bytes=16 * 1024 * 1024),
    )(vertical_taps, values)


def solution(mesh):
    return jax.shard_map(
        shards,
        mesh=mesh,
        in_specs=(P(None, "gy", "gx"), P(), P(None, "gy"), P()),
        out_specs=P(None, "gy", "gx"),
        check_vma=False,
    )
```
